1024 devices in a mesh: node: 64 (over x, y), feat: 16 (over z, core).
Axes of the slice: x: 8, y: 8, z: 8, core: 2. Of those that a mesh axis runs over, the one named last changes fastest.
Arguments:
- features: bfloat16 [16384, 768], P('node', 'feat'), may hold values from -6 to 6
- weight: bfloat16 [768, 1024], P('feat'), may hold values from -0.3125 to 0.3125
- tile_weights: bfloat16 [128, 8, 128, 128], P('node'), may hold values from -0.1875 to 0.1875
- tile_cols: int32 [128, 8], P('node'), may hold values from 0 to 127, as said below
- tile_count: int32 [128], P('node'), may hold values from 1 to 8, as said below
- out_grad: bfloat16 [16384, 1024], P('node', 'feat'), may hold values from -6 to 6
- relu_mask: int32 [16384, 1024], P('node', 'feat'), may hold values 0 or 1
Outputs:
- activations: bfloat16 [16384, 1024], P('node', 'feat')
- feature_grad: bfloat16 [16384, 768], P('node', 'feat')
The draws below stay inside these ranges and needn't reach their ends.
Inputs may be any that keep to these rules, and one draw needn't show every extreme that they name: `tile_cols`: the 8 column tiles of a row tile are distinct; the row tiles of one node block read at most 1 distinct column tiles of any one node block through used slots, and exactly 1 of some block in every node block. `tile_count`: every node block has a row tile with all 8 slots used.
All inputs are finite; a program needn't handle non-finite values. No bound on the sum of `relu_mask` on one device may be relied on, other than what follows from the above.
Results may differ from the reference program's by a relative error of at most 0.0049.
Values may be sent and summed in bfloat16 or wider, within the bound.
A program may use at most 32 MiB of HBM per device.

```python
import jax
import jax.numpy as jnp
from jax import lax

D_IN = 768
D_OUT = 1024
TILE = 128
TB = 2
K = 8
CAP = 1
BLOCKS = 64
NT = 128
NODES = 16384


def draw_tile_cols(key, part):
    key = jax.random.fold_in(key, 11)
    key_order, key_rotation, key_slots, key_picks = jax.random.split(key, 4)
    group_count = TB // CAP
    owner_order = jax.vmap(lambda subkey: jax.random.permutation(subkey, BLOCKS))(jax.random.split(key_order, BLOCKS))
    rotation = jax.random.randint(key_rotation, (BLOCKS, group_count), 0, BLOCKS)
    slot_perm = jax.vmap(lambda subkey: jax.random.permutation(subkey, CAP))(jax.random.split(key_slots, BLOCKS * group_count)).reshape(BLOCKS, group_count, CAP)
    tile_picks = jax.vmap(lambda subkey: jax.random.permutation(subkey, TB)[:CAP])(jax.random.split(key_picks, BLOCKS * BLOCKS)).reshape(BLOCKS, BLOCKS, CAP)
    block_index = jnp.arange(BLOCKS)[:, None, None]
    row_index = jnp.arange(TB)[None, :, None]
    slot_index = jnp.arange(K)[None, None, :]
    group_index = row_index // CAP
    position = (rotation[block_index, group_index] + slot_index) % BLOCKS
    owner_block = owner_order[block_index, position]
    pick_index = slot_perm[block_index, group_index, row_index % CAP]
    tile_pick = tile_picks[block_index, owner_block, pick_index]
    return (owner_block * TB + tile_pick).reshape(BLOCKS * TB, K).astype(jnp.int32)


def draw_tile_count(key, part):
    key = jax.random.fold_in(key, 12)
    key_heavy, key_full, key_light, key_top = jax.random.split(key, 4)
    heavy_block = jax.random.randint(key_heavy, (BLOCKS, 1), 0, 2)
    full_count = jax.random.randint(key_full, (BLOCKS, TB), 1, K + 1)
    light_count = jax.random.randint(key_light, (BLOCKS, TB), 1, K // 2 + 1)
    top_row = jax.random.randint(key_top, (BLOCKS, 1), 0, TB)
    row_counts = jnp.where(heavy_block == 1, full_count, light_count)
    row_counts = jnp.where(jnp.arange(TB)[None, :] == top_row, K, row_counts)
    return row_counts.reshape(BLOCKS * TB).astype(jnp.int32)


def touch_ends(array, stream_key, smallest, largest):
    place = [jax.random.randint(jax.random.fold_in(stream_key, axis), (), 0, length) for axis, length in enumerate(array.shape)]
    longest = array.shape.index(max(array.shape))
    beside = place[:longest] + [(place[longest] + 1) % array.shape[longest]] + place[longest + 1:]
    return array.at[tuple(place)].set(smallest).at[tuple(beside)].set(largest)


def raised(array, key, source, target, shards_of, factor):
    owner, partner = [(jnp.arange(array.shape[axis_at]) // (array.shape[axis_at] // shards_of)).reshape([-1 if axis == axis_at else 1 for axis in range(array.ndim)]) for axis_at in (source, target)]
    chosen = jax.random.permutation(key, shards_of)[partner]
    strong = (owner == chosen) | (owner == (partner + shards_of // 2) % shards_of)
    return jnp.where(strong, factor * array, array)


def block_levels(own_key, extent, pieces, low, largest):
    factor_of = 1.0
    for dim, blocks in pieces:
        draws = jax.random.uniform(jax.random.fold_in(jax.random.fold_in(own_key, 6), dim), (blocks,), jnp.float32, low / len(pieces), largest / len(pieces))
        factor_of = factor_of * jnp.repeat(jnp.exp(draws), extent[dim] // blocks).reshape((-1,) + (1,) * (len(extent) - 1 - dim))
    return factor_of


def gaussian(own_key, extent, spread, bound, pieces=(), kind=jnp.bfloat16):
    entries = jax.random.normal(own_key, extent, jnp.float32) * spread
    if len(pieces) > 0:
        entries = block_levels(own_key, extent, pieces, -0.22, 0.18) * entries
    return jnp.clip(entries, min=-bound, max=bound).astype(kind)


def heavy_noise(stream_key, dims, deviation, most, cuts, heavy, kind=jnp.bfloat16):
    array = deviation * jax.random.normal(stream_key, dims, jnp.float32)
    if cuts:
        array = array * block_levels(stream_key, dims, cuts, -0.22, 0.18)
    return jnp.clip(raised(array, jax.random.fold_in(stream_key, 3), *heavy), -most, most).astype(kind)


def setup_inputs(seed: int = 0) -> dict:
    key_list = jax.random.split(jax.random.key(seed), 8)
    features = gaussian(key_list[0], (NODES, D_IN), 1.0, 6.0, ((0, 64), (1, 16)))
    weight = heavy_noise(key_list[1], (D_IN, D_OUT), D_IN ** -0.5, 0.3125, ((0, 16),), (0, 1, 16, 2.0))
    tile_weights = gaussian(key_list[2], (NT, K, TILE, TILE), (K * TILE) ** -0.5, 0.1875, ((0, 64),))
    tile_cols = draw_tile_cols(jax.random.fold_in(key_list[7], 71), 0)
    tile_count = draw_tile_count(jax.random.fold_in(key_list[7], 71), 0)
    out_grad = gaussian(key_list[5], (NODES, D_OUT), 1.0, 6.0, ((0, 64), (1, 16)))
    relu_mask = touch_ends((jax.random.randint(key_list[6], (NODES, D_OUT), 0, 2) < 1).astype(jnp.int32), jax.random.fold_in(key_list[6], 1), 0, 1)
    return {"features": features, "weight": weight, "tile_weights": tile_weights, "tile_cols": tile_cols, "tile_count": tile_count, "out_grad": out_grad, "relu_mask": relu_mask}


def reference(features, weight, tile_weights, tile_cols, tile_count, out_grad, relu_mask):
    mixed = jnp.dot(features, weight, preferred_element_type=jnp.float32).astype(jnp.bfloat16)
    row_tiles = tile_cols.shape[0]
    mixed_tiles = mixed.reshape(row_tiles, TILE, D_OUT).astype(jnp.float32)
    valid_ref = (jnp.arange(K, dtype=jnp.int32)[None, :] < tile_count[:, None]).astype(jnp.float32)
    masked_grad = (out_grad * relu_mask.astype(jnp.bfloat16)).reshape(row_tiles, TILE, D_OUT).astype(jnp.float32)

    def accumulate(carried, slot_index):
        forward_sum, backward_sum = carried
        weights_now = jnp.take(tile_weights, slot_index, axis=1).astype(jnp.float32)
        weights_now = weights_now * jnp.take(valid_ref, slot_index, axis=1)[:, None, None]
        cols_now = jnp.take(tile_cols, slot_index, axis=1)
        forward_sum = forward_sum + jnp.einsum("tij,tjf->tif", weights_now, mixed_tiles[cols_now])
        backward_sum = backward_sum.at[cols_now].add(jnp.einsum("tij,tif->tjf", weights_now, masked_grad))
        return (forward_sum, backward_sum), None

    start_sums = (jnp.zeros((row_tiles, TILE, D_OUT), jnp.float32), jnp.zeros((row_tiles, TILE, D_OUT), jnp.float32))
    (forward_sum, backward_sum), _ = lax.scan(accumulate, start_sums, jnp.arange(K, dtype=jnp.int32))
    activations = jnp.maximum(forward_sum, 0.0).astype(jnp.bfloat16).reshape(row_tiles * TILE, D_OUT)
    back_sums = backward_sum.astype(jnp.bfloat16).reshape(row_tiles * TILE, D_OUT)
    feature_grad = jnp.dot(back_sums, weight.T, preferred_element_type=jnp.float32).astype(jnp.bfloat16)
    return activations, feature_grad
```

```python
import functools

import jax
import jax.numpy as jnp
from jax import lax
from jax.experimental import pallas as pl
from jax.experimental.pallas import tpu as pltpu
from jax.sharding import PartitionSpec as P

MESH = pl.DeviceIdType.MESH
R = 8
HALF = R // 2
U = 2
G = R // U
TILE = 128
UP, DOWN = 0, 1
STEP = (1, -1)
NEAR = (1, 7, 2, 6, 3, 5, 4)
NEAR_UNITS = (0, 3, 1, 2)
BF16, F32 = jnp.bfloat16, jnp.float32


def dot(a, b, dims=((1,), (0,))):
    return lax.dot_general(a, b, (dims, ((), ())), preferred_element_type=F32)


def kernel(
    source_ref, slot_ref, x_ref, w_ref, a_ref, g_ref, m_ref,
    act_ref, grad_ref,
    xall, first, parts, terms, kept, passed, landed, gall, zall, wall, wturn, outs,
    fs_recv, fh_recv, bh_recv, bs_recv, z_recv, sends,
):
    node, feat = lax.axis_index("node"), lax.axis_index("feat")
    x, y = node // R, lax.rem(node, R)
    z, core = feat // 2, lax.rem(feat, 2)
    din, dout = x_ref.shape[0], g_ref.shape[0]

    def on_first(t, d):
        if t == 0:
            return {"node": lax.rem(x + d + R, R) * R + y, "feat": feat}
        return {"node": x * R + lax.rem(y + d + R, R), "feat": feat}

    def on_ring(t, d):
        return on_first(1 - t, d)

    def on_z(d):
        return {"node": node, "feat": lax.rem(z + d, R) * 2 + core}

    partner = {"node": node, "feat": z * 2 + 1 - core}

    barrier = pltpu.get_barrier_semaphore()
    peers = [on_first(t, d) for t in (0, 1) for d in NEAR] + [on_z(d) for d in NEAR] + [partner]
    for peer in peers:
        pl.semaphore_signal(barrier, inc=1, device_id=peer, device_id_type=MESH)

    def place(t, e, d):
        return t * R * R + (e % R) * R + d % R

    def remote(src, dst, send_sem, recv_sem, to):
        return pltpu.make_async_remote_copy(
            src_ref=src, dst_ref=dst, send_sem=send_sem, recv_sem=recv_sem, device_id=to, device_id_type=MESH
        )

    def arrived(ref, sem):
        remote(ref, ref, sends.at[0], sem, partner).wait_recv()

    for t in (0, 1):
        xall[place(t, 0, 0)] = x_ref[:, t * TILE : (t + 1) * TILE]
    xall[2 * R * R] = jnp.zeros((din, TILE), BF16)
    for r in (0, 1):
        terms[r * 9 + 8] = jnp.zeros((din, TILE), F32)
    g_rows = lambda f: pl.ds(pl.multiple_of(f * dout, dout), dout)
    x_rows = lambda f: pl.ds(pl.multiple_of(f * din, din), din)
    gall[g_rows(feat), :] = g_ref[...] * m_ref[...].astype(BF16)
    columns = lambda zz: pl.ds(pl.multiple_of(zz * 2 * dout, 2 * dout), 2 * dout)
    wall[x_rows(feat), :] = w_ref[:, columns(z)]

    pl.semaphore_wait(barrier, len(peers))

    def z_start(k, buf, rows, source=None):
        for d in NEAR:
            src = buf.at[rows(feat), :] if source is None else source(lax.rem(z + d, R))
            remote(src, buf.at[rows(feat), :], sends.at[k], z_recv.at[k, feat], on_z(d)).start()
        remote(buf.at[rows(feat), :], buf.at[rows(feat), :], sends.at[k], z_recv.at[k, feat], partner).start()

    def z_forward(k, buf, rows):
        for d in NEAR:
            f = lax.rem(z - d + R, R) * 2 + core
            chunk = buf.at[rows(f), :]
            arrived(chunk, z_recv.at[k, f])
            remote(chunk, chunk, sends.at[k], z_recv.at[k, f], partner).start()

    def z_finish(k, buf, rows):
        for d in (0,) + NEAR:
            f = lax.rem(z - d + R, R) * 2 + 1 - core
            arrived(buf.at[rows(f), :], z_recv.at[k, f])

    def fs_start():
        for d in NEAR:
            for t in (0, 1):
                remote(
                    xall.at[place(t, 0, 0)], xall.at[place(t, 0, -d)], sends.at[3], fs_recv.at[t, -d % R], on_first(t, d)
                ).start()

    def fh_units(step, way):
        if step == HALF - 1:
            return [u for u in NEAR_UNITS if (u < G // 2) == (way == UP)]
        return NEAR_UNITS

    def fh_step(step):
        for place_at in range(G):
            for t in (0, 1):
                for way in (UP, DOWN):
                    units = fh_units(step, way)
                    if place_at >= len(units):
                        continue
                    u = units[place_at]
                    if step == 0 and way == UP:
                        for d in range(u * U, u * U + U):
                            if d:
                                arrived(xall.at[place(t, 0, d)], fs_recv.at[t, d])
                    chunk = xall.at[pl.ds(place(t, -STEP[way] * step, u * U), U)]
                    if step:
                        arrived(chunk, fh_recv.at[t, way, step - 1, u])
                    remote(
                        chunk,
                        xall.at[pl.ds(place(t, -STEP[way] * (step + 1), u * U), U)],
                        sends.at[3],
                        fh_recv.at[t, way, step, u],
                        on_ring(t, STEP[way]),
                    ).start()

    def fh_finish():
        for t in (0, 1):
            for way in (UP, DOWN):
                for step in (HALF - 2, HALF - 1):
                    for u in range(G):
                        if step == HALF - 2 and u in fh_units(HALF - 1, way):
                            continue
                        if step == HALF - 1 and u not in fh_units(step, way):
                            continue
                        chunk = xall.at[pl.ds(place(t, -STEP[way] * (step + 1), u * U), U)]
                        arrived(chunk, fh_recv.at[t, way, step, u])

    def aggregate():
        for r in (0, 1):
            total = jnp.zeros((din, TILE), F32)
            for k in range(8):
                total += dot(xall[source_ref[r, k]], a_ref[r, k], ((1,), (1,)))
            zall[x_rows(feat), r * TILE : (r + 1) * TILE] = total.astype(BF16)

    def finish_forward():
        result = dot(wturn[...], zall[...])
        outs[...] = jnp.maximum(result, 0.0)
        act_ref[...] = outs[pl.ds(pl.multiple_of(core * dout, dout), dout), :].astype(BF16)

    def make_terms():
        back = dot(w_ref[...], gall[...])
        high = back.astype(BF16)
        low = (back - high.astype(F32)).astype(BF16)
        both = jnp.concatenate([high, low], axis=0)
        for r in (0, 1):
            rows = both[:, r * TILE : (r + 1) * TILE]
            for k in range(8):
                term = dot(rows, a_ref[r, k])
                terms[r * 9 + k] = term[:din] + term[din:]

    def own(t, e, d):
        j = place(t, e, d)
        return terms[slot_ref[0, j]] + terms[slot_ref[1, j]]

    def part(t, way, step, u):
        return ((t * 2 + way) * HALF + step) * R + u * U

    def bh_units(step, way):
        if step == 0:
            return [u for u in range(G) if (u < G // 2) == (way == UP)]
        return range(G)

    def bh_step(step):
        for place_at in range(G):
            for t in (0, 1):
                for way in (UP, DOWN):
                    units = bh_units(step, way)
                    if place_at >= len(units):
                        continue
                    u = units[place_at]
                    e = STEP[way] * (HALF - step)
                    if step == 0:
                        ref, base = first, (t * G + u) * U
                    else:
                        ref, base = parts, part(t, way, step - 1, u)
                    coming = step > 1 or (step == 1 and u in bh_units(0, way))
                    chunk = ref.at[pl.ds(base, U)]
                    if coming:
                        arrived(chunk, bh_recv.at[t, way, step - 1, u])
                    for i in range(U):
                        value = own(t, e, u * U + i)
                        if coming:
                            value += ref[base + i].astype(F32)
                        ref[base + i] = value.astype(BF16)
                    remote(
                        chunk,
                        parts.at[pl.ds(part(t, way, step, u), U)],
                        sends.at[4],
                        bh_recv.at[t, way, step, u],
                        on_ring(t, STEP[way]),
                    ).start()

    def bs_start():
        for u in (0, 3, 1, 2):
            for t in (0, 1):
                for way in (UP, DOWN):
                    base = part(t, way, HALF - 1, u)
                    arrived(parts.at[pl.ds(base, U)], bh_recv.at[t, way, HALF - 1, u])
                for i in range(U):
                    d = u * U + i
                    value = own(t, 0, d)
                    for way in (UP, DOWN):
                        value += parts[part(t, way, HALF - 1, u) + i].astype(F32)
                    if d == 0:
                        kept[t] = value
                        continue
                    passed[t * R + d] = value.astype(BF16)
                    remote(
                        passed.at[t * R + d],
                        landed.at[t * R + (-d) % R],
                        sends.at[4],
                        bs_recv.at[t, -d % R],
                        on_first(t, d),
                    ).start()

    def bs_finish():
        for t in (0, 1):
            total = kept[t]
            for d in NEAR:
                arrived(landed.at[t * R + (-d) % R], bs_recv.at[t, -d % R])
                total += landed[t * R + (-d) % R].astype(F32)
            grad_ref[:, t * TILE : (t + 1) * TILE] = total.astype(BF16)

    fs_start()
    z_start(0, gall, g_rows)
    fh_step(0)
    z_start(1, wall, x_rows, lambda zz: w_ref.at[:, columns(zz)])
    fh_step(1)
    z_forward(0, gall, g_rows)
    fh_step(2)
    z_finish(0, gall, g_rows)
    fh_step(3)
    make_terms()
    bh_step(0)
    bh_step(1)
    fh_finish()
    aggregate()
    z_start(2, zall, x_rows)
    z_forward(1, wall, x_rows)
    bh_step(2)
    z_forward(2, zall, x_rows)
    bh_step(3)
    z_finish(1, wall, x_rows)
    wturn[...] = wall[...].T
    bs_start()
    z_finish(2, zall, x_rows)
    finish_forward()
    bs_finish()

    def left(ref, count, sem):
        for _ in range(count):
            remote(ref, ref, sem, z_recv.at[0, 0], partner).wait_send()

    z_bytes = [buf.at[pl.ds(0, (2 * R - 1) * rows), :] for buf, rows in ((gall, dout), (wall, din), (zall, din))]
    for k in range(3):
        left(z_bytes[k], 1, sends.at[k])
    left(xall.at[pl.ds(0, 2 * (R - 1) * (R + 1))], 1, sends.at[3])
    left(parts.at[pl.ds(0, 2 * (R - 1) * (R + 1))], 1, sends.at[4])


def local(features, weight, tile_weights, tile_cols, tile_count, out_grad, relu_mask):
    din, dout = features.shape[1], out_grad.shape[1]
    rows = features.shape[0]
    node = lax.axis_index("node")
    x, y = node // R, node % R
    block, t = tile_cols // 2, tile_cols % 2
    dx, dy = (block // R - x) % R, (block % R - y) % R
    where = jnp.where(t == 0, dy * R + dx, R * R + dx * R + dy)
    slots = jnp.arange(8, dtype=jnp.int32)[None, :]
    source = jnp.where(slots < tile_count[:, None], where, 2 * R * R).astype(jnp.int32)
    hits = source[:, :, None] == jnp.arange(2 * R * R, dtype=jnp.int32)[None, None, :]
    slot = jnp.sum(jnp.where(hits, slots[:, :, None] - 8, 0), axis=1) + 8
    slot = slot + 9 * jnp.arange(2, dtype=jnp.int32)[:, None]

    vmem = pl.BlockSpec(memory_space=pltpu.VMEM)
    smem = pl.BlockSpec(memory_space=pltpu.SMEM)
    dma = pltpu.SemaphoreType.DMA
    act, grad = pl.pallas_call(
        kernel,
        out_shape=(
            jax.ShapeDtypeStruct((dout, rows), BF16),
            jax.ShapeDtypeStruct((din, rows), BF16),
        ),
        in_specs=[smem, smem, vmem, vmem, vmem, vmem, vmem],
        out_specs=(vmem, vmem),
        scratch_shapes=[
            pltpu.VMEM((2 * R * R + 1, din, TILE), BF16),
            pltpu.VMEM((2 * R, din, TILE), BF16),
            pltpu.VMEM((4 * HALF * R, din, TILE), BF16),
            pltpu.VMEM((18, din, TILE), F32),
            pltpu.VMEM((2, din, TILE), F32),
            pltpu.VMEM((2 * R, din, TILE), BF16),
            pltpu.VMEM((2 * R, din, TILE), BF16),
            pltpu.VMEM((2 * R * dout, rows), BF16),
            pltpu.VMEM((2 * R * din, rows), BF16),
            pltpu.VMEM((2 * R * din, 2 * dout), BF16),
            pltpu.VMEM((2 * dout, 2 * R * din), BF16),
            pltpu.VMEM((2 * dout, rows), F32),
            dma((2, R)),
            dma((2, 2, HALF, G)),
            dma((2, 2, HALF, G)),
            dma((2, R)),
            dma((3, 2 * R)),
            dma((5,)),
        ],
        compiler_params=pltpu.CompilerParams(
            collective_id=0, has_side_effects=True, vmem_limit_bytes=24 * 1024 * 1024
        ),
        name="graph_layer",
    )(source, slot, features.T, weight, tile_weights, out_grad.T, relu_mask.T)
    return act.T, grad.T


def solution(mesh):
    in_specs = (
        P("node", "feat"),
        P("feat", None),
        P("node", None, None, None),
        P("node", None),
        P("node"),
        P("node", "feat"),
        P("node", "feat"),
    )
    out_specs = (P("node", "feat"), P("node", "feat"))
    return jax.shard_map(local, mesh=mesh, in_specs=in_specs, out_specs=out_specs, check_vma=False)
```

```python
import jax
import jax.numpy as jnp
from jax import lax
from jax.experimental import pallas as pl
from jax.experimental.pallas import tpu as pltpu
from jax.sharding import PartitionSpec as P

MESH = pl.DeviceIdType.MESH
R = 8
TILE = 128
SLOTS = 8
BOTH = (0, 1)
OWN, OTHER = 0, 1
FAR = (4, 3, 5, 2, 6, 1, 7)
NEAR = FAR[::-1]
PER = R // 2
PART = PER // 2
SOURCES = ((1, 7, 3, 5), (0, 6, 2, 4))
LINES = 2 * R * PER
BF16, F32 = jnp.bfloat16, jnp.float32


def dot(a, b, dims=((1,), (0,))):
    return lax.dot_general(a, b, (dims, ((), ())), preferred_element_type=F32)


def back(axis, d):
    return (axis if d % 2 == 0 else 1 - axis), -d % R


def line(axis, d):
    return axis * R + d


def kernel(
    x_hbm, w_hbm, a_hbm, cols_hbm, count_hbm, g_hbm, m_hbm,
    act_ref, grad_ref,
    w_ref, a_ref, g_ref, m_ref, cols_ref, count_ref, table, slot_ref,
    asked, wanted, tiles, picked, got, terms, sent, back_in, kept, passed, landed, gall, zall, wall, wturn, outs,
    local_sem, q_recv, s_recv, h_recv, b_recv, l_recv, z_recv, w_recv, sends,
):
    node, feat = lax.axis_index("node"), lax.axis_index("feat")
    x, y = node // R, lax.rem(node, R)
    z, core = feat // 2, lax.rem(feat, 2)
    odd_block = lax.rem(x + y, 2)
    din, dout = x_hbm.shape[0], g_hbm.shape[0]

    def on_line(axis, d):
        along_x = lax.rem(x + d, R) * R + y
        along_y = x * R + lax.rem(y + d, R)
        use_y = odd_block if axis == OWN else 1 - odd_block
        return {"node": along_x + use_y * (along_y - along_x), "feat": feat}

    def on_z(d):
        return {"node": node, "feat": lax.rem(z + d + R, R) * 2 + core}

    partner = {"node": node, "feat": z * 2 + 1 - core}

    barrier = pltpu.get_barrier_semaphore()
    peers = [to for d in FAR for to in (on_line(OWN, d), on_line(OTHER, d), on_z(d))] + [partner]
    for peer in peers:
        pl.semaphore_signal(barrier, inc=1, device_id=peer, device_id_type=MESH)

    def fetch(src, dst, i):
        copy = pltpu.make_async_copy(src, dst, local_sem.at[i])
        copy.start()
        return copy

    get_cols, get_count = fetch(cols_hbm, cols_ref, 4), fetch(count_hbm, count_ref, 5)
    get_g, get_m = fetch(g_hbm, g_ref, 2), fetch(m_hbm, m_ref, 3)
    get_x = [fetch(x_hbm.at[:, pl.ds(t * TILE, TILE)], tiles.at[0, t], t) for t in BOTH]
    get_w, get_a = fetch(w_hbm, w_ref, 6), fetch(a_hbm, a_ref, 7)

    def remote(src, dst, send_sem, recv_sem, to):
        return pltpu.make_async_remote_copy(
            src_ref=src, dst_ref=dst, send_sem=send_sem, recv_sem=recv_sem, device_id=to, device_id_type=MESH
        )

    def arrived(ref, sem):
        remote(ref, ref, sends.at[0], sem, partner).wait_recv()

    g_rows = lambda f: pl.ds(pl.multiple_of(f * dout, dout), dout)
    x_rows = lambda f: pl.ds(pl.multiple_of(f * din, din), din)
    columns = lambda zz: pl.ds(pl.multiple_of(zz * 2 * dout, 2 * dout), 2 * dout)

    got[LINES] = jnp.zeros((din, TILE), BF16)
    for r in BOTH:
        terms[r * (SLOTS + 1) + SLOTS] = jnp.zeros((din, TILE), F32)

    get_cols.wait()
    get_count.wait()
    lanes = lax.broadcasted_iota(jnp.int32, (1, TILE), 1)
    rows = lax.broadcasted_iota(jnp.int32, asked.shape, 0)
    flags = jnp.zeros(asked.shape, jnp.int32)
    source = []
    for r in BOTH:
        row = jnp.full((1, TILE), r * (SLOTS + 1) + SLOTS, jnp.int32)
        for k in range(SLOTS):
            col = cols_ref[r, k]
            block = col >> 1
            bx, by = block >> 3, jnp.bitwise_and(block, R - 1)
            dx, dy = jnp.bitwise_and(bx - x + R, R - 1), jnp.bitwise_and(by - y + R, R - 1)
            odd = jnp.bitwise_and(bx + by, 1)
            d, i = jnp.where(odd == 1, dx, dy), jnp.where(odd == 1, dy, dx) >> 1
            i = jnp.where(i == 0, 0, jnp.where(i == 3, 1, i + 1))
            axis = jnp.where(odd == odd_block, OTHER, OWN)
            at = (axis * R + d) * PER + i
            used = k < count_ref[r]
            source.append(jnp.where(used, at, LINES))
            row = jnp.where(lanes == jnp.where(used, at, -1), r * (SLOTS + 1) + k, row)
            second = jnp.logical_and(used, jnp.bitwise_and(col, 1) == 1)
            flags = jnp.where(rows == jnp.where(second, (axis * R + d) * 8 + i, -1), 1, flags)
        table[r : r + 1, :] = row
    asked[...] = flags
    get_slot = fetch(table, slot_ref, 4)
    for axis in BOTH:
        mine = slice(line(axis, 0) * 8, line(axis, 0) * 8 + 8)
        wanted[mine, :] = flags[mine, :]
    get_g.wait()
    get_m.wait()
    gall[g_rows(feat), :] = g_ref[...] * m_ref[...].astype(BF16)
    get_w.wait()
    wall[x_rows(feat), :] = w_ref[:, columns(z)]
    for copy in get_x:
        copy.wait()

    pl.semaphore_wait(barrier, len(peers))

    def z_start(k, buf, rows):
        mine = buf.at[rows(feat), :]
        for to in [on_z(d) for d in FAR] + [partner]:
            remote(mine, mine, sends.at[k], z_recv.at[k, feat], to).start()

    def z_pass(k, buf, rows, distances):
        for d in distances:
            f = lax.rem(z + d, R) * 2 + core
            chunk = buf.at[rows(f), :]
            arrived(chunk, z_recv.at[k, f])
            remote(chunk, chunk, sends.at[k], z_recv.at[k, f], partner).start()

    def z_finish(k, buf, rows):
        for d in FAR + (0,):
            f = lax.rem(z + d, R) * 2 + 1 - core
            arrived(buf.at[rows(f), :], z_recv.at[k, f])

    def w_start():
        mine = x_rows(feat)
        for d in FAR:
            src = w_ref.at[:, columns(lax.rem(z + d, R))]
            remote(src, wall.at[mine, :], sends.at[2], w_recv.at[feat], on_z(d)).start()
        remote(wall.at[mine, :], wall.at[mine, :], sends.at[2], w_recv.at[feat], partner).start()

    def w_forward():
        for d in range(1, R):
            f = lax.rem(z + d, R) * 2 + core
            chunk = wall.at[x_rows(f), :]
            arrived(chunk, w_recv.at[f])
            remote(chunk, chunk, sends.at[2], w_recv.at[f], partner).start()

    def w_finish():
        for d in range(R):
            f = lax.rem(z + d, R) * 2 + 1 - core
            arrived(wall.at[x_rows(f), :], w_recv.at[f])
        wturn[...] = wall[...].T

    def ask():
        for d in FAR:
            for axis in BOTH:
                there, e = back(axis, d)
                remote(
                    asked.at[pl.ds(line(axis, d) * 8, 8), :],
                    wanted.at[pl.ds(line(there, e) * 8, 8), :],
                    sends.at[3],
                    q_recv.at[there, e],
                    on_line(axis, d),
                ).start()

    def spread():
        for d in FAR:
            remote(tiles.at[0], tiles.at[-d % R], sends.at[4], s_recv.at[-d % R], on_line(OWN, d)).start()

    def second_wanted(axis, d, i):
        row = line(axis, d) * 8 + i
        return wanted[row : row + 1, :] == 1

    def pick(axis, d, to, i):
        two = tiles[SOURCES[axis][i]].astype(F32)
        to[line(axis, d) * PER + i] = jnp.where(second_wanted(axis, d, i), two[1], two[0]).astype(BF16)

    def part(axis, d, half):
        return pl.ds(line(axis, d) * PER + half * PART, PART)

    def pass_on(half, order):
        blocks = range(half * PART, half * PART + PART)
        for axis in BOTH:
            for i in blocks:
                d = SOURCES[axis][i]
                if d:
                    arrived(tiles.at[d], s_recv.at[d])
        for d in order:
            for axis in BOTH:
                there, e = back(axis, d)
                if half == 0:
                    arrived(wanted.at[pl.ds(line(axis, d) * 8, 8), :], q_recv.at[axis, d])
                for i in blocks:
                    pick(axis, d, picked, i)
                remote(
                    picked.at[part(axis, d, half)],
                    got.at[part(there, e, half)],
                    sends.at[5],
                    h_recv.at[there, e, half],
                    on_line(axis, d),
                ).start()
        for axis in BOTH:
            for i in blocks:
                pick(axis, 0, got, i)

    def have_all():
        for half in BOTH:
            for axis in BOTH:
                for d in FAR:
                    arrived(got.at[part(axis, d, half)], h_recv.at[axis, d, half])

    def aggregate():
        for r in BOTH:
            total = jnp.zeros((din, TILE), F32)
            for k in range(SLOTS):
                total += dot(got[source[r * SLOTS + k]], a_ref[r, k], ((1,), (1,)))
            zall[x_rows(feat), r * TILE : (r + 1) * TILE] = total.astype(BF16)

    def finish_forward():
        outs[...] = jnp.maximum(dot(wturn[...], zall[...]), 0.0)
        act_ref[...] = outs[pl.ds(pl.multiple_of(core * dout, dout), dout), :].astype(BF16)

    def make_terms():
        back = dot(w_ref[...], gall[...])
        high = back.astype(BF16)
        low = (back - high.astype(F32)).astype(BF16)
        both = jnp.concatenate([high, low], axis=0)
        for r in BOTH:
            rows = both[:, r * TILE : (r + 1) * TILE]
            for k in range(SLOTS):
                term = dot(rows, a_ref[r, k])
                terms[r * (SLOTS + 1) + k] = term[:din] + term[din:]

    def own(axis, d, i):
        j = line(axis, d) * PER + i
        return terms[slot_ref[0, j]] + terms[slot_ref[1, j]]

    def send_terms(half):
        for d in FAR:
            for axis in BOTH:
                there, e = back(axis, d)
                for i in range(half * PART, half * PART + PART):
                    sent[line(axis, d) * PER + i] = own(axis, d, i).astype(BF16)
                remote(
                    sent.at[part(axis, d, half)],
                    back_in.at[part(there, e, half)],
                    sends.at[6],
                    b_recv.at[there, e, half],
                    on_line(axis, d),
                ).start()

    def sum_terms(half):
        for axis in BOTH:
            for d in FAR:
                arrived(back_in.at[part(axis, d, half)], b_recv.at[axis, d, half])
        for i in reversed(range(half * PART, half * PART + PART)):
            for axis in (OTHER, OWN):
                d = SOURCES[axis][i]
                totals = [jnp.zeros((din, TILE), F32) for _ in BOTH]
                for e in (0,) + FAR:
                    value = back_in[line(axis, e) * PER + i].astype(F32) if e else own(axis, 0, i)
                    second = second_wanted(axis, e, i)
                    totals[0] += jnp.where(second, 0.0, value)
                    totals[1] += jnp.where(second, value, 0.0)
                for t in BOTH:
                    if d:
                        passed[d, t] = totals[t].astype(BF16)
                    else:
                        kept[t] = totals[t]
                if d:
                    there = OWN if d % 2 == 0 else OTHER
                    remote(
                        passed.at[d], landed.at[-d % R], sends.at[7], l_recv.at[-d % R], on_line(there, d)
                    ).start()

    def finish_backward():
        totals = [kept[t] for t in BOTH]
        for d in FAR:
            arrived(landed.at[d], l_recv.at[d])
            for t in BOTH:
                totals[t] += landed[d, t].astype(F32)
        for t in BOTH:
            grad_ref[:, t * TILE : (t + 1) * TILE] = totals[t].astype(BF16)

    grads, mixes = (0, gall, g_rows), (1, zall, x_rows)
    ask()
    z_start(*grads)
    spread()
    pass_on(0, FAR)
    z_pass(*grads, FAR[:3])
    pass_on(1, FAR)
    z_pass(*grads, FAR[3:])
    get_a.wait()
    get_slot.wait()
    z_finish(*grads)
    make_terms()
    send_terms(1)
    send_terms(0)
    w_start()
    have_all()
    aggregate()
    z_start(*mixes)
    w_forward()
    sum_terms(1)
    z_pass(*mixes, FAR)
    sum_terms(0)
    w_finish()
    z_finish(*mixes)
    finish_forward()
    finish_backward()

    for buf, n, k in (
        (gall, (2 * R - 1) * dout, 0),
        (zall, (2 * R - 1) * din, 1),
        (wall, (2 * R - 1) * din, 2),
        (asked, 2 * (R - 1) * 8, 3),
        (picked, 2 * (R - 1) * PER, 5),
        (sent, 2 * (R - 1) * PER, 6),
        (tiles, R - 1, 4),
        (passed, R - 1, 7),
    ):
        ref = buf.at[pl.ds(0, n)]
        remote(ref, ref, sends.at[k], w_recv.at[0], partner).wait_send()


def local(features, weight, tile_weights, tile_cols, tile_count, out_grad, relu_mask):
    din, dout = features.shape[1], out_grad.shape[1]
    rows = features.shape[0]
    vmem = pl.BlockSpec(memory_space=pltpu.VMEM)
    hbm = pl.BlockSpec(memory_space=pltpu.HBM)
    dma = pltpu.SemaphoreType.DMA
    act, grad = pl.pallas_call(
        kernel,
        out_shape=(
            pltpu.VMEM((dout, rows), BF16),
            pltpu.VMEM((din, rows), BF16),
        ),
        in_specs=[hbm] * 7,
        out_specs=(vmem, vmem),
        scratch_shapes=[
            pltpu.VMEM(weight.shape, BF16),
            pltpu.VMEM(tile_weights.shape, BF16),
            pltpu.VMEM((dout, rows), BF16),
            pltpu.VMEM((dout, rows), jnp.int32),
            pltpu.SMEM(tile_cols.shape, jnp.int32),
            pltpu.SMEM(tile_count.shape, jnp.int32),
            pltpu.VMEM((2, TILE), jnp.int32),
            pltpu.SMEM((2, TILE), jnp.int32),
            pltpu.VMEM((2 * R * 8, TILE), jnp.int32),
            pltpu.VMEM((2 * R * 8, TILE), jnp.int32),
            pltpu.VMEM((R, 2, din, TILE), BF16),
            pltpu.VMEM((LINES, din, TILE), BF16),
            pltpu.VMEM((LINES + 1, din, TILE), BF16),
            pltpu.VMEM((2 * (SLOTS + 1), din, TILE), F32),
            pltpu.VMEM((LINES, din, TILE), BF16),
            pltpu.VMEM((LINES, din, TILE), BF16),
            pltpu.VMEM((2, din, TILE), F32),
            pltpu.VMEM((R, 2, din, TILE), BF16),
            pltpu.VMEM((R, 2, din, TILE), BF16),
            pltpu.VMEM((2 * R * dout, rows), BF16),
            pltpu.VMEM((2 * R * din, rows), BF16),
            pltpu.VMEM((2 * R * din, 2 * dout), BF16),
            pltpu.VMEM((2 * dout, 2 * R * din), BF16),
            pltpu.VMEM((2 * dout, rows), F32),
            dma((8,)),
            dma((2, R)),
            dma((R,)),
            dma((2, R, 2)),
            dma((2, R, 2)),
            dma((R,)),
            dma((2, 2 * R)),
            dma((2 * R,)),
            dma((8,)),
        ],
        compiler_params=pltpu.CompilerParams(
            collective_id=0, has_side_effects=True, vmem_limit_bytes=60 * 1024 * 1024
        ),
        name="graph_layer",
    )(features.T, weight, tile_weights, tile_cols, tile_count, out_grad.T, relu_mask.T)
    return act.T, grad.T


def solution(mesh):
    in_specs = (
        P("node", "feat"),
        P("feat", None),
        P("node", None, None, None),
        P("node", None),
        P("node"),
        P("node", "feat"),
        P("node", "feat"),
    )
    out_specs = (P("node", "feat"), P("node", "feat"))
    return jax.shard_map(local, mesh=mesh, in_specs=in_specs, out_specs=out_specs, check_vma=False)
```

```python
import jax
import jax.numpy as jnp
from jax import lax
from jax.experimental import pallas as pl
from jax.experimental.pallas import tpu as pltpu
from jax.sharding import PartitionSpec as P

MESH = pl.DeviceIdType.MESH
R = 8
TILE = 128
SLOTS = 8
BOTH = (0, 1)
OWN, OTHER = 0, 1
FAR = (4, 3, 5, 2, 6, 1, 7)
NEAR = FAR[::-1]
PER = R // 2
PART = PER // 2
SOURCES = ((1, 7, 3, 5), (0, 6, 2, 4))
LINES = 2 * R * PER
BF16, F32 = jnp.bfloat16, jnp.float32


def dot(a, b, dims=((1,), (0,))):
    return lax.dot_general(a, b, (dims, ((), ())), preferred_element_type=F32)


def back(axis, d):
    return (axis if d % 2 == 0 else 1 - axis), -d % R


def line(axis, d):
    return axis * R + d


def kernel(
    x_hbm, w_hbm, a_hbm, cols_hbm, count_hbm, g_hbm, m_hbm,
    act_ref, grad_ref,
    w_ref, a_ref, g_ref, m_ref, cols_ref, count_ref, table, slot_ref,
    asked, wanted, tiles, picked, got, terms, sent, back_in, kept, passed, landed, gall, zall, wall, wturn, outs,
    local_sem, q_recv, s_recv, h_recv, b_recv, l_recv, z_recv, w_recv, sends,
):
    node, feat = lax.axis_index("node"), lax.axis_index("feat")
    x, y = node // R, lax.rem(node, R)
    z, core = feat // 2, lax.rem(feat, 2)
    odd_block = lax.rem(x + y, 2)
    din, dout = x_hbm.shape[0], g_hbm.shape[0]

    def on_line(axis, d):
        along_x = lax.rem(x + d, R) * R + y
        along_y = x * R + lax.rem(y + d, R)
        use_y = odd_block if axis == OWN else 1 - odd_block
        return {"node": along_x + use_y * (along_y - along_x), "feat": feat}

    def on_z(d):
        return {"node": node, "feat": lax.rem(z + d + R, R) * 2 + core}

    partner = {"node": node, "feat": z * 2 + 1 - core}

    barrier = pltpu.get_barrier_semaphore()
    peers = [to for d in FAR for to in (on_line(OWN, d), on_line(OTHER, d), on_z(d))] + [partner]
    for peer in peers:
        pl.semaphore_signal(barrier, inc=1, device_id=peer, device_id_type=MESH)

    def fetch(src, dst, i):
        copy = pltpu.make_async_copy(src, dst, local_sem.at[i])
        copy.start()
        return copy

    get_cols, get_count = fetch(cols_hbm, cols_ref, 4), fetch(count_hbm, count_ref, 5)
    get_g, get_m = fetch(g_hbm, g_ref, 2), fetch(m_hbm, m_ref, 3)
    get_x = [fetch(x_hbm.at[:, pl.ds(t * TILE, TILE)], tiles.at[0, t], t) for t in BOTH]
    get_w, get_a = fetch(w_hbm, w_ref, 6), fetch(a_hbm, a_ref, 7)

    def remote(src, dst, send_sem, recv_sem, to):
        return pltpu.make_async_remote_copy(
            src_ref=src, dst_ref=dst, send_sem=send_sem, recv_sem=recv_sem, device_id=to, device_id_type=MESH
        )

    def arrived(ref, sem):
        remote(ref, ref, sends.at[0], sem, partner).wait_recv()

    g_rows = lambda f: pl.ds(pl.multiple_of(f * dout, dout), dout)
    x_rows = lambda f: pl.ds(pl.multiple_of(f * din, din), din)
    columns = lambda zz: pl.ds(pl.multiple_of(zz * 2 * dout, 2 * dout), 2 * dout)

    got[LINES] = jnp.zeros((din, TILE), BF16)
    for r in BOTH:
        terms[r * (SLOTS + 1) + SLOTS] = jnp.zeros((din, TILE), F32)

    get_cols.wait()
    get_count.wait()
    lanes = lax.broadcasted_iota(jnp.int32, (1, TILE), 1)
    rows = lax.broadcasted_iota(jnp.int32, asked.shape, 0)
    flags = jnp.zeros(asked.shape, jnp.int32)
    source = []
    for r in BOTH:
        row = jnp.full((1, TILE), r * (SLOTS + 1) + SLOTS, jnp.int32)
        for k in range(SLOTS):
            col = cols_ref[r, k]
            block = col >> 1
            bx, by = block >> 3, jnp.bitwise_and(block, R - 1)
            dx, dy = jnp.bitwise_and(bx - x + R, R - 1), jnp.bitwise_and(by - y + R, R - 1)
            odd = jnp.bitwise_and(bx + by, 1)
            d, i = jnp.where(odd == 1, dx, dy), jnp.where(odd == 1, dy, dx) >> 1
            i = jnp.where(i == 0, 0, jnp.where(i == 3, 1, i + 1))
            axis = jnp.where(odd == odd_block, OTHER, OWN)
            at = (axis * R + d) * PER + i
            used = k < count_ref[r]
            source.append(jnp.where(used, at, LINES))
            row = jnp.where(lanes == jnp.where(used, at, -1), r * (SLOTS + 1) + k, row)
            second = jnp.logical_and(used, jnp.bitwise_and(col, 1) == 1)
            flags = jnp.where(rows == jnp.where(second, (axis * R + d) * 8 + i, -1), 1, flags)
        table[r : r + 1, :] = row
    asked[...] = flags
    get_slot = fetch(table, slot_ref, 4)
    for axis in BOTH:
        mine = slice(line(axis, 0) * 8, line(axis, 0) * 8 + 8)
        wanted[mine, :] = flags[mine, :]
    get_g.wait()
    get_m.wait()
    gall[g_rows(feat), :] = g_ref[...] * m_ref[...].astype(BF16)
    get_w.wait()
    wall[x_rows(feat), :] = w_ref[:, columns(z)]
    for copy in get_x:
        copy.wait()

    pl.semaphore_wait(barrier, len(peers))

    def z_start(k, buf, rows):
        mine = buf.at[rows(feat), :]
        for to in [on_z(d) for d in FAR] + [partner]:
            remote(mine, mine, sends.at[k], z_recv.at[k, feat], to).start()

    def z_pass(k, buf, rows, distances):
        for d in distances:
            f = lax.rem(z + d, R) * 2 + core
            chunk = buf.at[rows(f), :]
            arrived(chunk, z_recv.at[k, f])
            remote(chunk, chunk, sends.at[k], z_recv.at[k, f], partner).start()

    def z_finish(k, buf, rows):
        for d in FAR + (0,):
            f = lax.rem(z + d, R) * 2 + 1 - core
            arrived(buf.at[rows(f), :], z_recv.at[k, f])

    def w_start():
        mine = x_rows(feat)
        for d in FAR:
            src = w_ref.at[:, columns(lax.rem(z + d, R))]
            remote(src, wall.at[mine, :], sends.at[2], w_recv.at[feat], on_z(d)).start()
        remote(wall.at[mine, :], wall.at[mine, :], sends.at[2], w_recv.at[feat], partner).start()

    def w_forward():
        for d in range(1, R):
            f = lax.rem(z + d, R) * 2 + core
            chunk = wall.at[x_rows(f), :]
            arrived(chunk, w_recv.at[f])
            remote(chunk, chunk, sends.at[2], w_recv.at[f], partner).start()

    def w_finish():
        for d in range(R):
            f = lax.rem(z + d, R) * 2 + 1 - core
            arrived(wall.at[x_rows(f), :], w_recv.at[f])
        wturn[...] = wall[...].T

    def ask():
        for d in FAR:
            for axis in BOTH:
                there, e = back(axis, d)
                remote(
                    asked.at[pl.ds(line(axis, d) * 8, 8), :],
                    wanted.at[pl.ds(line(there, e) * 8, 8), :],
                    sends.at[3],
                    q_recv.at[there, e],
                    on_line(axis, d),
                ).start()

    def spread():
        for d in NEAR:
            remote(tiles.at[0], tiles.at[-d % R], sends.at[4], s_recv.at[-d % R], on_line(OWN, d)).start()

    def second_wanted(axis, d, i):
        row = line(axis, d) * 8 + i
        return wanted[row : row + 1, :] == 1

    def pick(axis, d, to, i):
        two = tiles[SOURCES[axis][i]].astype(F32)
        to[line(axis, d) * PER + i] = jnp.where(second_wanted(axis, d, i), two[1], two[0]).astype(BF16)

    def part(axis, d, half):
        return pl.ds(line(axis, d) * PER + half * PART, PART)

    def pass_on(half, order):
        blocks = range(half * PART, half * PART + PART)
        for axis in BOTH:
            for i in blocks:
                d = SOURCES[axis][i]
                if d:
                    arrived(tiles.at[d], s_recv.at[d])
        for d in order:
            for axis in BOTH:
                there, e = back(axis, d)
                if half == 0:
                    arrived(wanted.at[pl.ds(line(axis, d) * 8, 8), :], q_recv.at[axis, d])
                for i in blocks:
                    pick(axis, d, picked, i)
                remote(
                    picked.at[part(axis, d, half)],
                    got.at[part(there, e, half)],
                    sends.at[5],
                    h_recv.at[there, e, half],
                    on_line(axis, d),
                ).start()
        for axis in BOTH:
            for i in blocks:
                pick(axis, 0, got, i)

    def have_all():
        for half in BOTH:
            for axis in BOTH:
                for d in FAR:
                    arrived(got.at[part(axis, d, half)], h_recv.at[axis, d, half])

    def aggregate():
        for r in BOTH:
            total = jnp.zeros((din, TILE), F32)
            for k in range(SLOTS):
                total += dot(got[source[r * SLOTS + k]], a_ref[r, k], ((1,), (1,)))
            zall[x_rows(feat), r * TILE : (r + 1) * TILE] = total.astype(BF16)

    def finish_forward():
        outs[...] = jnp.maximum(dot(wturn[...], zall[...]), 0.0)
        act_ref[...] = outs[pl.ds(pl.multiple_of(core * dout, dout), dout), :].astype(BF16)

    def make_terms():
        back = dot(w_ref[...], gall[...])
        high = back.astype(BF16)
        low = (back - high.astype(F32)).astype(BF16)
        both = jnp.concatenate([high, low], axis=0)
        for r in BOTH:
            rows = both[:, r * TILE : (r + 1) * TILE]
            for k in range(SLOTS):
                term = dot(rows, a_ref[r, k])
                terms[r * (SLOTS + 1) + k] = term[:din] + term[din:]

    def own(axis, d, i):
        j = line(axis, d) * PER + i
        return terms[slot_ref[0, j]] + terms[slot_ref[1, j]]

    def send_terms(half):
        for d in FAR:
            for axis in BOTH:
                there, e = back(axis, d)
                for i in range(half * PART, half * PART + PART):
                    sent[line(axis, d) * PER + i] = own(axis, d, i).astype(BF16)
                remote(
                    sent.at[part(axis, d, half)],
                    back_in.at[part(there, e, half)],
                    sends.at[6],
                    b_recv.at[there, e, half],
                    on_line(axis, d),
                ).start()

    def sum_terms(half):
        for axis in BOTH:
            for d in FAR:
                arrived(back_in.at[part(axis, d, half)], b_recv.at[axis, d, half])
        for i in reversed(range(half * PART, half * PART + PART)):
            for axis in (OTHER, OWN):
                d = SOURCES[axis][i]
                totals = [jnp.zeros((din, TILE), F32) for _ in BOTH]
                for e in (0,) + FAR:
                    value = back_in[line(axis, e) * PER + i].astype(F32) if e else own(axis, 0, i)
                    second = second_wanted(axis, e, i)
                    totals[0] += jnp.where(second, 0.0, value)
                    totals[1] += jnp.where(second, value, 0.0)
                for t in BOTH:
                    if d:
                        passed[d, t] = totals[t].astype(BF16)
                    else:
                        kept[t] = totals[t]
                if d:
                    there = OWN if d % 2 == 0 else OTHER
                    remote(
                        passed.at[d], landed.at[-d % R], sends.at[7], l_recv.at[-d % R], on_line(there, d)
                    ).start()

    def finish_backward():
        totals = [kept[t] for t in BOTH]
        for d in FAR:
            arrived(landed.at[d], l_recv.at[d])
            for t in BOTH:
                totals[t] += landed[d, t].astype(F32)
        for t in BOTH:
            grad_ref[:, t * TILE : (t + 1) * TILE] = totals[t].astype(BF16)

    grads, mixes = (0, gall, g_rows), (1, zall, x_rows)
    ask()
    spread()
    z_start(*grads)
    pass_on(0, FAR)
    pass_on(1, FAR)
    z_pass(*grads, FAR)
    get_a.wait()
    get_slot.wait()
    z_finish(*grads)
    make_terms()
    send_terms(1)
    send_terms(0)
    w_start()
    have_all()
    aggregate()
    z_start(*mixes)
    w_forward()
    sum_terms(1)
    z_pass(*mixes, FAR)
    sum_terms(0)
    w_finish()
    z_finish(*mixes)
    finish_forward()
    finish_backward()

    for buf, n, k in (
        (gall, (2 * R - 1) * dout, 0),
        (zall, (2 * R - 1) * din, 1),
        (wall, (2 * R - 1) * din, 2),
        (asked, 2 * (R - 1) * 8, 3),
        (picked, 2 * (R - 1) * PER, 5),
        (sent, 2 * (R - 1) * PER, 6),
        (tiles, R - 1, 4),
        (passed, R - 1, 7),
    ):
        ref = buf.at[pl.ds(0, n)]
        remote(ref, ref, sends.at[k], w_recv.at[0], partner).wait_send()


def local(features, weight, tile_weights, tile_cols, tile_count, out_grad, relu_mask):
    din, dout = features.shape[1], out_grad.shape[1]
    rows = features.shape[0]
    vmem = pl.BlockSpec(memory_space=pltpu.VMEM)
    hbm = pl.BlockSpec(memory_space=pltpu.HBM)
    dma = pltpu.SemaphoreType.DMA
    act, grad = pl.pallas_call(
        kernel,
        out_shape=(
            pltpu.VMEM((dout, rows), BF16),
            pltpu.VMEM((din, rows), BF16),
        ),
        in_specs=[hbm] * 7,
        out_specs=(vmem, vmem),
        scratch_shapes=[
            pltpu.VMEM(weight.shape, BF16),
            pltpu.VMEM(tile_weights.shape, BF16),
            pltpu.VMEM((dout, rows), BF16),
            pltpu.VMEM((dout, rows), jnp.int32),
            pltpu.SMEM(tile_cols.shape, jnp.int32),
            pltpu.SMEM(tile_count.shape, jnp.int32),
            pltpu.VMEM((2, TILE), jnp.int32),
            pltpu.SMEM((2, TILE), jnp.int32),
            pltpu.VMEM((2 * R * 8, TILE), jnp.int32),
            pltpu.VMEM((2 * R * 8, TILE), jnp.int32),
            pltpu.VMEM((R, 2, din, TILE), BF16),
            pltpu.VMEM((LINES, din, TILE), BF16),
            pltpu.VMEM((LINES + 1, din, TILE), BF16),
            pltpu.VMEM((2 * (SLOTS + 1), din, TILE), F32),
            pltpu.VMEM((LINES, din, TILE), BF16),
            pltpu.VMEM((LINES, din, TILE), BF16),
            pltpu.VMEM((2, din, TILE), F32),
            pltpu.VMEM((R, 2, din, TILE), BF16),
            pltpu.VMEM((R, 2, din, TILE), BF16),
            pltpu.VMEM((2 * R * dout, rows), BF16),
            pltpu.VMEM((2 * R * din, rows), BF16),
            pltpu.VMEM((2 * R * din, 2 * dout), BF16),
            pltpu.VMEM((2 * dout, 2 * R * din), BF16),
            pltpu.VMEM((2 * dout, rows), F32),
            dma((8,)),
            dma((2, R)),
            dma((R,)),
            dma((2, R, 2)),
            dma((2, R, 2)),
            dma((R,)),
            dma((2, 2 * R)),
            dma((2 * R,)),
            dma((8,)),
        ],
        compiler_params=pltpu.CompilerParams(
            collective_id=0, has_side_effects=True, vmem_limit_bytes=60 * 1024 * 1024
        ),
        name="graph_layer",
    )(features.T, weight, tile_weights, tile_cols, tile_count, out_grad.T, relu_mask.T)
    return act.T, grad.T


def solution(mesh):
    in_specs = (
        P("node", "feat"),
        P("feat", None),
        P("node", None, None, None),
        P("node", None),
        P("node"),
        P("node", "feat"),
        P("node", "feat"),
    )
    out_specs = (P("node", "feat"), P("node", "feat"))
    return jax.shard_map(local, mesh=mesh, in_specs=in_specs, out_specs=out_specs, check_vma=False)
```
